256 devices in a mesh: pipe: 8 (over y, core), dp: 32 (over x, z).
Axes of the slice: x: 4, y: 4, z: 8, core: 2. Of those that a mesh axis runs over, the one named last changes fastest.
Arguments:
- embedded: bfloat16 [4, 1024, 6144], P(None, 'dp'), may hold values from -6 to 6
- out_grads: bfloat16 [8, 4, 1024, 6144], P('pipe', None, 'dp'), may hold values from -6 to 6
- section_gains: float32 [8, 6144], P('pipe'), may hold values from 0.25 to 1.75
- plan: int32 [8, 2], replicated, may hold values from 0 to 7, as said below
Outputs:
- normed_inputs: float32 [8, 4, 1024, 6144], P('pipe', None, 'dp')
- inverse_factors: float32 [8, 1536, 1536], P('pipe', 'dp')
The draws below stay inside these ranges and needn't reach their ends.
Inputs may be any that keep to these rules, and one draw needn't show every extreme that they name: `plan`: column 0 is a block id 0 to 2 * 4 - 1 (ids under 4 name blocks of normed_inputs, the others blocks of out_grads); column 1 is a permutation of the sections.
All inputs are finite; a program needn't handle non-finite values.
Results may differ from the reference program's by a relative error of at most 0.0012.
Values sent between devices are 32-bit elements; how exact they have to be, the bound alone decides.
No kernel may reach another device: no remote copies, remote signals or barrier semaphores. Data moves between devices by JAX's collectives and lax.ppermute only.
A program may use at most 192 MiB of HBM per device.

```python
import jax
import jax.numpy as jnp
from jax import lax

D = 6144
BLK = 1536
MB = 4
NB = 4
TOKENS = 1024
N_PIPE = 8


def draw_plan(key, part):
    key = jax.random.fold_in(key, 7)
    first_key, second_key, third_key = jax.random.split(key, 3)
    block_ids = jax.random.randint(first_key, (N_PIPE,), 0, 2 * NB)
    top_place = jax.random.randint(third_key, (), 0, N_PIPE)
    block_ids = jnp.where(jnp.arange(N_PIPE) == top_place, 2 * NB - 1, block_ids)
    target_ids = jax.random.permutation(second_key, N_PIPE)
    return jnp.stack([block_ids, target_ids], axis=1).astype(jnp.int32)


def steps_of(rng, dims, cuts, low, largest):
    def one(position, parts):
        steps = jax.random.uniform(jax.random.fold_in(jax.random.fold_in(rng, 6), position), (parts,), jnp.float32, low / len(cuts), largest / len(cuts))
        return jnp.repeat(jnp.exp(steps), dims[position] // parts).reshape((-1,) + (1,) * (len(dims) - position - 1))

    loudness = one(*cuts[0])
    for cut in cuts[1:]:
        loudness = loudness * one(*cut)
    return loudness


def centred(own_key, shape, width, bound, cuts=(), kind=jnp.bfloat16):
    loudness = steps_of(own_key, shape, cuts, -0.22, 0.18) if cuts else 1.0
    result = jax.random.normal(own_key, shape, jnp.float32) * width * loudness
    return jnp.minimum(jnp.maximum(result, -bound), bound).astype(kind)


def setup_inputs(seed: int = 0) -> dict:
    streams_of = jax.random.split(jax.random.key(seed), 5)
    embedded = centred(streams_of[0], (MB, TOKENS, D), 1.0, 6.0, ((1, 32),))
    out_grads = centred(streams_of[1], (N_PIPE, MB, TOKENS, D), 1.0, 6.0, ((0, 8), (2, 32)))
    section_gains = jnp.clip(1.0 + 0.15 * jax.random.normal(streams_of[2], (N_PIPE, D), jnp.float32), 0.25, 1.75)
    plan = draw_plan(jax.random.fold_in(streams_of[4], 71), 0)
    return {"embedded": embedded, "out_grads": out_grads, "section_gains": section_gains, "plan": plan}


damping_term = 0.1

def section_norm(hidden, gain_row):
    scale = lax.rsqrt(lax.optimization_barrier(jnp.mean(hidden * hidden, axis=-1, keepdims=True)) + 1e-05)
    return hidden * scale * gain_row

def reference(embedded, out_grads, section_gains, plan):
    hidden = embedded.astype(jnp.float32)
    normed_list = []
    for section_pos in range(N_PIPE):
        normed = section_norm(hidden, section_gains[section_pos])
        normed_list.append(normed)
        hidden = hidden + jax.nn.silu(normed)
    normed_all = jnp.stack(normed_list, axis=0)
    identity_block = jnp.eye(BLK, dtype=jnp.float32)
    inverse_list = []
    for section_pos in range(N_PIPE):
        both_sides = jnp.concatenate([normed_all[section_pos].astype(jnp.bfloat16), out_grads[section_pos]], axis=-1)
        both_sides = both_sides.reshape(MB * TOKENS, 2 * D)
        col_start = (plan[section_pos, 0] * BLK).astype(jnp.int32)
        columns = lax.dynamic_slice_in_dim(both_sides, col_start, BLK, 1)
        covariance = jnp.dot(columns.T.astype(jnp.float32), columns.astype(jnp.float32), preferred_element_type=jnp.float32) / (MB * TOKENS)
        covariance = covariance + damping_term * identity_block
        factor_low = jnp.linalg.cholesky(covariance)
        inverse = lax.linalg.triangular_solve(factor_low, identity_block, left_side=True, lower=True)
        inverse_list.append(inverse)
    return (normed_all, jnp.stack(inverse_list, axis=0))
```

```python
import jax
import jax.numpy as jnp
from jax import lax
from jax.experimental import pallas as pl
from jax.experimental.pallas import tpu as pltpu
from jax.sharding import PartitionSpec as P

BLK = 1536
B = 128
NBK = BLK // B
DAMPING = 0.1
EPS = 1e-5
CHUNK = 512

f32 = jnp.float32
bf16 = jnp.bfloat16


def split(x):
    high = x.astype(bf16)
    low = (x - high.astype(f32)).astype(bf16)
    return high, low


def dot(a, b):
    return jnp.dot(a, b, preferred_element_type=f32)


def dot3(a, b):
    return dot(a[0], b[0]) + dot(a[1], b[0]) + dot(a[0], b[1])


def packed_place(k):
    return (k, 0) if k < NBK // 2 else (NBK - 1 - k, k + 1)


def relay_body(
    scalars, embedded_ref, gains_ref, grads_ref, normed_ref, packed_ref, hidden_ref, columns_ref
):
    section = scalars[0]
    block_id = scalars[1]
    step = pl.program_id(0)
    rows, width = hidden_ref.shape
    spans = [(start, CHUNK) for start in range(0, width, CHUNK)]

    def squares(total, h):
        square = h * h
        for lane in range(0, CHUNK, 128):
            total = total + square[:, lane : lane + 128]
        return total

    def scale_of(total):
        mean = jnp.sum(total, axis=1, keepdims=True) * (1.0 / width)
        return jnp.broadcast_to(lax.rsqrt(mean + EPS), (rows, CHUNK))

    total = jnp.zeros((rows, 128), f32)
    for start, size in spans:
        h = embedded_ref[0, :, start : start + size].astype(f32)
        hidden_ref[:, start : start + size] = h
        total = squares(total, h)

    def one_section(s, total):
        scale = scale_of(total)
        total = jnp.zeros((rows, 128), f32)
        for start, size in spans:
            h = hidden_ref[:, start : start + size]
            gain = gains_ref[pl.ds(s, 1), start : start + size]
            half = h * scale * (gain * 0.5)
            h = h + (half + half * jnp.tanh(half))
            hidden_ref[:, start : start + size] = h
            total = squares(total, h)
        return total

    total = lax.fori_loop(0, section, one_section, total)
    scale = scale_of(total)
    for start, size in spans:
        h = hidden_ref[:, start : start + size]
        gain = gains_ref[pl.ds(section, 1), start : start + size]
        normed_ref[0, 0, :, start : start + size] = h * scale * gain

    row = pl.multiple_of(step * rows, rows)

    @pl.when(block_id < width // BLK)
    def _():
        place = pl.multiple_of(block_id * BLK, BLK)
        columns_ref[pl.ds(row, rows), :] = normed_ref[0, 0, :, pl.ds(place, BLK)].astype(bf16)

    @pl.when(block_id >= width // BLK)
    def _():
        columns_ref[pl.ds(row, rows), :] = grads_ref[0, 0]

    @pl.when(step == pl.num_programs(0) - 1)
    def _():
        columns = columns_ref[...]
        for k in range(NBK):
            place, first = packed_place(k)
            left = columns[:, k * B : (k + 1) * B].T
            packed_ref[place * B : (place + 1) * B, first * B : (first + NBK - k) * B] = dot(
                left, columns[:, k * B :]
            )


def relay(scalars, embedded, gains, grads):
    micro, rows, width = embedded.shape
    sections = gains.shape[0]
    blocks = width // BLK
    return pl.pallas_call(
        relay_body,
        grid_spec=pltpu.PrefetchScalarGridSpec(
            num_scalar_prefetch=1,
            grid=(micro,),
            in_specs=[
                pl.BlockSpec((1, rows, width), lambda m, sc: (m, 0, 0)),
                pl.BlockSpec((sections, width), lambda m, sc: (0, 0)),
                pl.BlockSpec(
                    (1, 1, rows, BLK), lambda m, sc: (0, m, 0, jnp.maximum(sc[1] - blocks, 0))
                ),
            ],
            out_specs=[
                pl.BlockSpec((1, 1, rows, width), lambda m, sc: (0, m, 0, 0)),
                pl.BlockSpec((BLK // 2, BLK + B), lambda m, sc: (0, 0)),
            ],
            scratch_shapes=[
                pltpu.VMEM((rows, width), f32),
                pltpu.VMEM((micro * rows, BLK), bf16),
            ],
        ),
        out_shape=[
            jax.ShapeDtypeStruct((1, micro, rows, width), f32),
            jax.ShapeDtypeStruct((BLK // 2, BLK + B), f32),
        ],
        compiler_params=pltpu.CompilerParams(vmem_limit_bytes=40 * 2**20),
    )(scalars, embedded, gains, grads)


def across_rows(x, j):
    return jnp.broadcast_to(x[j : j + 1, :], x.shape)


def across_lanes(x, j):
    return jnp.broadcast_to(x[:, j : j + 1], x.shape)


def reciprocal(p):
    r = pl.reciprocal(p, approx=True)
    return r * (2.0 - p * r)


def inverse_factor(d):
    sub = lax.broadcasted_iota(jnp.int32, (8, 128), 0)
    lane = lax.broadcasted_iota(jnp.int32, (8, 128), 1)
    rows = [d[8 * i : 8 * i + 8, :] for i in range(16)]
    for t in range(8):
        top, low = rows[2 * t], rows[2 * t + 1]
        top_cols = [across_lanes(top, 16 * t + j) for j in range(16)]
        low_cols = [across_lanes(low, 16 * t + j) for j in range(16)]
        own = (lane >= 16 * t) & (lane < 16 * t + 16)
        top = jnp.where(own, (lane - 16 * t == sub).astype(f32), top)
        low = jnp.where(own, (lane - 16 * t - 8 == sub).astype(f32), low)
        top_pivots = jnp.zeros((8, 128), f32)
        low_pivots = top_pivots
        for j in range(16):
            if j < 8:
                pivot = across_rows(top_cols[j], j)
                r = reciprocal(pivot)
                top_pivots = jnp.where(sub == j, pivot, top_pivots)
                top_mult = jnp.where(sub > j, top_cols[j] * r, 0.0)
                low_mult = low_cols[j] * r
                for q in range(j + 1, 16):
                    s = across_rows(top_cols[q], j)
                    top_cols[q] = top_cols[q] - top_mult * s
                    low_cols[q] = low_cols[q] - low_mult * s
                s = across_rows(top, j)
                top = top - top_mult * s
                low = low - low_mult * s
            else:
                i = j - 8
                pivot = across_rows(low_cols[j], i)
                low_pivots = jnp.where(sub == i, pivot, low_pivots)
                if i < 7:
                    r = reciprocal(pivot)
                    low_mult = jnp.where(sub > i, low_cols[j] * r, 0.0)
                    for q in range(j + 1, 16):
                        low_cols[q] = low_cols[q] - low_mult * across_rows(low_cols[q], i)
                    low = low - low_mult * across_rows(low, i)
        top = top * lax.rsqrt(top_pivots)
        low = low * lax.rsqrt(low_pivots)
        rows[2 * t], rows[2 * t + 1] = top, low
        if t < 7:
            strip = jnp.concatenate([top, low], 0)
            high, rest = split(strip)
            turned_high, turned_rest = split(strip.T)
            update = dot(
                jnp.concatenate([turned_high, turned_high, turned_rest], 1),
                jnp.concatenate([high, rest, high], 0),
            )
            for i in range(2 * t + 2, 16):
                rows[i] = jnp.where(own, 0.0, rows[i]) - update[8 * i : 8 * i + 8, :]
    return jnp.concatenate(rows, 0)


def factor_body(tokens, first_row, packed_ref, out_ref, work):
    lane = lax.broadcasted_iota(jnp.int32, (B, B), 1)
    sub = lax.broadcasted_iota(jnp.int32, (B, B), 0)
    for k in range(NBK):
        place, first = packed_place(k)
        rows = slice(k * B, (k + 1) * B)
        work[rows, k * B :] = packed_ref[
            place * B : (place + 1) * B, first * B : (first + NBK - k) * B
        ] * (1.0 / tokens)
        work[rows, rows] = work[rows, rows] + jnp.where(lane == sub, DAMPING, 0.0)
    for k in range(NBK):
        done = k * B
        rows = slice(done, done + B)
        w = jnp.where(lane <= sub, inverse_factor(work[rows, rows]), 0.0)
        new = dot3(split(w), split(work[rows, :]))
        work[rows, :] = new
        work[rows, rows] = w
        if k + 1 == NBK:
            break
        turned_high, turned_low = split(work[rows, done + B :].T)
        high, low = split(work[rows, :])
        for i in range(k + 1, NBK):
            at = slice((i - k - 1) * B, (i - k) * B)
            left = (turned_high[at], turned_low[at])
            target = slice(i * B, (i + 1) * B)
            x = dot3(left, (high[:, : done + B], low[:, : done + B]))
            if k:
                work[target, :done] = work[target, :done] - x[:, :done]
            work[target, rows] = -x[:, done:]
            y = dot3(left, (high[:, i * B :], low[:, i * B :]))
            work[target, i * B :] = work[target, i * B :] - y
    count = out_ref.shape[1]
    start = pl.multiple_of(first_row[0], 8)
    out_lane = lax.broadcasted_iota(jnp.int32, (count, BLK), 1)
    out_row = lax.broadcasted_iota(jnp.int32, (count, BLK), 0) + start
    out_ref[0] = jnp.where(out_lane <= out_row, work[pl.ds(start, count), :], 0.0)


def factor(packed, first_row, count, tokens):
    return pl.pallas_call(
        lambda *refs: factor_body(tokens, *refs),
        out_shape=jax.ShapeDtypeStruct((1, count, BLK), f32),
        in_specs=[
            pl.BlockSpec(memory_space=pltpu.SMEM),
            pl.BlockSpec(memory_space=pltpu.VMEM),
        ],
        out_specs=pl.BlockSpec(memory_space=pltpu.VMEM),
        scratch_shapes=[pltpu.VMEM((BLK, BLK), f32)],
        compiler_params=pltpu.CompilerParams(vmem_limit_bytes=50 * 2**20),
    )(first_row, packed)


def on_device(embedded, out_grads, section_gains, plan):
    section = lax.axis_index("pipe")
    data_count = lax.axis_size("dp")
    data_index = lax.axis_index("dp")
    micro, rows, _ = embedded.shape
    gains = lax.all_gather(section_gains, "pipe", axis=0, tiled=True)
    scalars = jnp.stack([section, plan[section, 0]]).astype(jnp.int32)
    normed, packed = relay(scalars, embedded, gains, out_grads)
    packed = lax.psum(packed, "dp")
    count = BLK // data_count
    first_row = (data_index * count).astype(jnp.int32)[None]
    own_rows = factor(packed, first_row, count, micro * rows * data_count)
    return normed, own_rows


def solution(mesh):
    in_specs = (P(None, "dp", None), P("pipe", None, "dp", None), P("pipe", None), P())
    out_specs = (P("pipe", None, "dp", None), P("pipe", "dp", None))
    return jax.shard_map(
        on_device, mesh=mesh, in_specs=in_specs, out_specs=out_specs, check_vma=False
    )
```

```python
import jax
import jax.numpy as jnp
from jax import lax
from jax.experimental import pallas as pl
from jax.experimental.pallas import tpu as pltpu
from jax.sharding import PartitionSpec as P

BLK = 1536
B = 128
CHUNKS = 4
W = BLK // CHUNKS
HALF = BLK // 2
EARLY, LATE = (0, 1), (2, 3)
DAMPING = 0.1
EPS = 1e-5
VMEM = 40 * 2**20
SPAN = 512

f32 = jnp.float32
bf16 = jnp.bfloat16


def split(x):
    high = x.astype(bf16)
    low = (x - high.astype(f32)).astype(bf16)
    return high, low


def dot(a, b):
    return jnp.dot(a, b, preferred_element_type=f32)


def dot3(a, b):
    return dot(a[0], b[0]) + dot(a[1], b[0]) + dot(a[0], b[1])


def dot3_nt(a, b):
    def one(x, y):
        return lax.dot_general(x, y, (((1,), (1,)), ((), ())), preferred_element_type=f32)

    return one(a[0], b[0]) + one(a[1], b[0]) + one(a[0], b[1])


def relay_body(
    plan, embedded_ref, gains_ref, grads_ref, normed_ref, left_ref, right_ref, hidden_ref
):
    section = lax.axis_index("pipe")
    block_id = plan[section, 0]
    rows, width = hidden_ref.shape
    spans = [(start, SPAN) for start in range(0, width, SPAN)]

    def squares(total, h):
        square = h * h
        for lane in range(0, SPAN, 128):
            total = total + square[:, lane : lane + 128]
        return total

    def scale_of(total):
        mean = jnp.sum(total, axis=1, keepdims=True) * (1.0 / width)
        return jnp.broadcast_to(lax.rsqrt(mean + EPS), (rows, SPAN))

    total = jnp.zeros((rows, 128), f32)
    for start, size in spans:
        h = embedded_ref[0, :, start : start + size].astype(f32)
        hidden_ref[:, start : start + size] = h
        total = squares(total, h)

    def one_section(s, total):
        scale = scale_of(total)
        total = jnp.zeros((rows, 128), f32)
        for start, size in spans:
            h = hidden_ref[:, start : start + size]
            gain = gains_ref[s, :, start : start + size]
            half = h * scale * (gain * 0.5)
            h = h + (half + half * jnp.tanh(half))
            hidden_ref[:, start : start + size] = h
            total = squares(total, h)
        return total

    total = lax.fori_loop(0, section, one_section, total)
    scale = scale_of(total)
    for start, size in spans:
        h = hidden_ref[:, start : start + size]
        gain = gains_ref[section, :, start : start + size]
        normed_ref[0, 0, :, start : start + size] = h * scale * gain

    for first, ref in ((0, left_ref), (HALF, right_ref)):

        @pl.when(block_id < width // BLK)
        def _():
            place = pl.multiple_of(block_id * BLK + first, HALF)
            ref[...] = normed_ref[0, 0, :, pl.ds(place, HALF)]

        @pl.when(block_id >= width // BLK)
        def _():
            ref[...] = grads_ref[0, 0, :, first : first + HALF].astype(f32)


def relay(plan, embedded, gains, grads):
    micro, rows, width = embedded.shape
    sections = gains.shape[0]
    blocks = width // BLK

    def grads_block(m, plan):
        return 0, m, 0, jnp.maximum(plan[lax.axis_index("pipe"), 0] - blocks, 0)

    return pl.pallas_call(
        relay_body,
        grid_spec=pltpu.PrefetchScalarGridSpec(
            num_scalar_prefetch=1,
            grid=(micro,),
            in_specs=[
                pl.BlockSpec((1, rows, width), lambda m, plan: (m, 0, 0)),
                pl.BlockSpec((sections, 1, width), lambda m, plan: (0, 0, 0)),
                pl.BlockSpec((1, 1, rows, BLK), grads_block),
            ],
            out_specs=[
                pl.BlockSpec((1, 1, rows, width), lambda m, plan: (0, m, 0, 0)),
                pl.BlockSpec((rows, HALF), lambda m, plan: (m, 0)),
                pl.BlockSpec((rows, HALF), lambda m, plan: (m, 0)),
            ],
            scratch_shapes=[pltpu.VMEM((rows, width), f32)],
        ),
        out_shape=[
            jax.ShapeDtypeStruct((1, micro, rows, width), f32),
            jax.ShapeDtypeStruct((micro * rows, HALF), f32),
            jax.ShapeDtypeStruct((micro * rows, HALF), f32),
        ],
        compiler_params=pltpu.CompilerParams(vmem_limit_bytes=VMEM),
    )(plan, embedded, gains, grads)


def tiles_of(c):
    for block in range(W // B):
        for group in range(B // 8 // CHUNKS):
            for tile in range(c * W // B + block + 1):
                yield block, group, tile


def tile_count(chunks):
    return sum(len(list(tiles_of(c))) for c in chunks)


def tiles_each(chunks, members):
    return -(-tile_count(chunks) // members)


def slab_member(members):
    index = lax.axis_index("dp")
    return lax.div(index, members), lax.rem(index, members)


def covariance_body(chunks, members, *refs):
    early = chunks == EARLY
    left_refs, right_refs = refs[:CHUNKS], refs[CHUNKS : 2 * CHUNKS]
    turned = refs[-1]
    if early:
        right_refs = ()
        copy_ref, *out_refs, tiles_ref = refs[CHUNKS + 1 : -1]
        copy_ref[...] = refs[CHUNKS][...]
    else:
        (tiles_ref,) = refs[2 * CHUNKS : -1]
    columns = [
        jnp.concatenate([ref[...] for ref in half], 0) for half in (left_refs, right_refs) if half
    ]
    turned[...] = columns[-1].T.reshape(turned.shape)
    slab, member = slab_member(members)
    left = turned[:, slab]
    groups, eight, tokens = left.shape
    left = left.reshape(groups * eight, tokens).astype(bf16)
    products = [dot(left, half.astype(bf16)) for half in columns]
    per_block = B // 8 // CHUNKS
    index = 0
    for c in chunks:
        for block, group, tile in tiles_of(c):
            row = 8 * (((c - chunks[0]) * (W // B) + block) * per_block + group)
            half, lane = divmod(tile * B, HALF)
            tiles_ref[index] = products[half][row : row + 8, lane : lane + B]
            index += 1
    if early:
        each = out_refs[0].shape[0]
        tiles_ref[index:] = jnp.zeros((each * members - index, 8, B), f32)
        for steps, ref in enumerate(out_refs):
            first = lax.rem(member + steps, members) * each
            ref[...] = tiles_ref[pl.ds(first, each)]


def covariance(chunks, lefts, rights, members):
    tokens = len(lefts) * lefts[0].shape[0]
    vmem = pl.BlockSpec(memory_space=pltpu.VMEM)
    scratch = [pltpu.VMEM((HALF // 8 // CHUNKS, CHUNKS, 8, tokens), f32)]
    if chunks == EARLY:
        each = tiles_each(chunks, members)
        out_shape = [jax.ShapeDtypeStruct(rights[0].shape, f32)]
        out_shape += [jax.ShapeDtypeStruct((each, 8, B), f32)] * members
        scratch.insert(0, pltpu.VMEM((each * members, 8, B), f32))
    else:
        out_shape = [jax.ShapeDtypeStruct((tile_count(chunks), 8, B), f32)]
    return pl.pallas_call(
        lambda *refs: covariance_body(chunks, members, *refs),
        out_shape=out_shape,
        in_specs=[vmem] * (len(lefts) + len(rights)),
        out_specs=[vmem] * len(out_shape),
        scratch_shapes=scratch,
        compiler_params=pltpu.CompilerParams(vmem_limit_bytes=VMEM),
    )(*lefts, *rights)


def fold_body(count, *refs):
    part_refs, out_ref = refs[:count], refs[-1]
    total = part_refs[0][...]
    for ref in part_refs[1:]:
        total = total + ref[...]
    out_ref[...] = total


def fold(parts, *after):
    vmem = pl.BlockSpec(memory_space=pltpu.VMEM)
    return pl.pallas_call(
        lambda *refs: fold_body(len(parts), *refs),
        out_shape=jax.ShapeDtypeStruct(parts[0].shape, f32),
        in_specs=[vmem] * len(parts) + [pl.BlockSpec(memory_space=pl.ANY)] * len(after),
        out_specs=vmem,
    )(*parts, *after)


def lay_body(members, *refs):
    *part_refs, out_ref = refs
    _, member = slab_member(members)
    for steps, ref in enumerate(part_refs):
        out_ref[lax.rem(member + (members - steps), members)] = ref[...]


def lay(parts):
    members = len(parts)
    vmem = pl.BlockSpec(memory_space=pltpu.VMEM)
    return pl.pallas_call(
        lambda *refs: lay_body(members, *refs),
        out_shape=jax.ShapeDtypeStruct((members, *parts[0].shape), f32),
        in_specs=[vmem] * members,
        out_specs=vmem,
    )(*parts)


def later_body(first, tiles_ref, *refs):
    out_ref = refs[-1]
    out_ref[...] = tiles_ref[first : first + out_ref.shape[0]]


def later(tiles, c, after):
    vmem = pl.BlockSpec(memory_space=pltpu.VMEM)
    return pl.pallas_call(
        lambda *refs: later_body(tile_count(range(LATE[0], c)), *refs),
        out_shape=jax.ShapeDtypeStruct((tile_count([c]), 8, B), f32),
        in_specs=[vmem] + [pl.BlockSpec(memory_space=pl.ANY)] * len(after),
        out_specs=vmem,
    )(tiles, *after)


def across_rows(x, j):
    return jnp.broadcast_to(x[j : j + 1, :], x.shape)


def across_lanes(x, j):
    return jnp.broadcast_to(x[:, j : j + 1], x.shape)


def reciprocal(p):
    r = pl.reciprocal(p, approx=True)
    return r * (2.0 - p * r)


def inverse_factor(d):
    sub = lax.broadcasted_iota(jnp.int32, (8, 128), 0)
    lane = lax.broadcasted_iota(jnp.int32, (8, 128), 1)
    rows = [d[8 * i : 8 * i + 8, :] for i in range(16)]
    for t in range(8):
        pair = [rows[2 * t], rows[2 * t + 1]]
        cols = [[across_lanes(x, 16 * t + j) for j in range(16)] for x in pair]
        own = (lane >= 16 * t) & (lane < 16 * t + 16)
        for half in range(2):
            one = (lane - 16 * t - 8 * half == sub).astype(f32)
            pair[half] = jnp.where(own, one, pair[half])
        scales = []
        for half in range(2):
            pivots = jnp.zeros((8, 128), f32)
            mine = cols[half]
            for i in range(0, 8, 2):
                j = 8 * half + i
                x, y = mine[j], mine[j + 1]
                a, b, c = across_rows(x, i), across_rows(y, i), across_rows(y, i + 1)
                det = a * c - b * b
                r = pl.reciprocal(det, approx=True)
                fix = 2.0 - det * r
                ra = reciprocal(a)
                pivots = jnp.where(sub == i, a, jnp.where(sub == i + 1, det * ra, pivots))
                within = jnp.where(sub == i + 1, b * ra, 0.0)
                first, second = across_rows(pair[half], i), across_rows(pair[half], i + 1)
                if i < 6:
                    below = sub > i + 1
                    m0 = jnp.where(below, (x * c - y * b) * r, 0.0) * fix
                    m1 = jnp.where(below, (y * a - x * b) * r, 0.0) * fix
                if half == 0:
                    x, y = cols[1][j], cols[1][j + 1]
                    n0 = (x * c - y * b) * r * fix
                    n1 = (y * a - x * b) * r * fix
                for q in range(j + 2, 16):
                    s0, s1 = across_rows(mine[q], i), across_rows(mine[q], i + 1)
                    if i < 6:
                        mine[q] = mine[q] - (m0 * s0 + m1 * s1)
                    if half == 0:
                        cols[1][q] = cols[1][q] - (n0 * s0 + n1 * s1)
                if i < 6:
                    pair[half] = pair[half] - ((m0 + within) * first + m1 * second)
                else:
                    pair[half] = pair[half] - within * first
                if half == 0:
                    pair[1] = pair[1] - (n0 * first + n1 * second)
            scales.append(lax.rsqrt(pivots))
        done = [pair[half] * scales[half] for half in range(2)]
        rows[2 * t], rows[2 * t + 1] = done
        if t < 7:
            left = split(jnp.concatenate(pair, 0))
            right = split(jnp.concatenate([done[half] * scales[half] for half in range(2)], 0))
            update = lax.dot_general(
                jnp.concatenate([left[0], left[0], left[1]], 0),
                jnp.concatenate([right[0], right[1], right[0]], 0),
                (((0,), (0,)), ((), ())),
                preferred_element_type=f32,
            )
            for i in range(2 * t + 2, 16):
                rows[i] = jnp.where(own, 0.0, rows[i]) - update[8 * i : 8 * i + 8, :]
    return jnp.concatenate(rows, 0)


def eliminate(work):
    size = work.shape[0]
    lane = lax.broadcasted_iota(jnp.int32, (B, B), 1)
    sub = lax.broadcasted_iota(jnp.int32, (B, B), 0)
    for done in range(0, size, B):
        rows = slice(done, done + B)
        w = jnp.where(lane <= sub, inverse_factor(work[rows, rows]), 0.0)
        new = dot3(split(w), split(work[rows, :]))
        work[rows, :] = new
        work[rows, rows] = w
        if done + B == size:
            break
        turned_high, turned_low = split(work[rows, done + B :].T)
        high, low = split(work[rows, :])
        for start in range(done + B, size, B):
            at = slice(start - done - B, start - done)
            left = (turned_high[at], turned_low[at])
            target = slice(start, start + B)
            x = dot3(left, (high[:, : done + B], low[:, : done + B]))
            if done:
                work[target, :done] = work[target, :done] - x[:, :done]
            work[target, rows] = -x[:, done:]
            y = dot3(left, (high[:, start:], low[:, start:]))
            work[target, start:] = work[target, start:] - y


def factor_body(c, first, tokens, members, *refs):
    last = c == CHUNKS - 1
    share_refs = refs[:CHUNKS]
    *before, out_ref, work, rows_ref = refs[CHUNKS:]
    slab, member = slab_member(members)
    for steps, ref in enumerate(share_refs):
        x = lax.rem(slab + (CHUNKS - steps), CHUNKS)
        for index, (block, group, tile) in enumerate(tiles_of(c)):
            row = pl.multiple_of(8 * x + (block * B + 8 * CHUNKS * group), 8)
            rows_ref[pl.ds(row, 8), tile * B : (tile + 1) * B] = ref[first + index]
    for block in range(W // B):
        for other in range(block):
            low = rows_ref[block * B : (block + 1) * B, c * W + other * B : c * W + (other + 1) * B]
            at = c * W + block * B
            rows_ref[other * B : (other + 1) * B, at : at + B] = low.T
    lane = lax.broadcasted_iota(jnp.int32, (W, W), 1)
    sub = lax.broadcasted_iota(jnp.int32, (W, W), 0)
    scale = 1.0 / tokens
    block = rows_ref[:, c * W :] * scale + jnp.where(lane == sub, DAMPING, 0.0)
    parts = []
    if c:
        row = split(rows_ref[:, : c * W] * scale)
        halves = [split(ref[...]) for ref in before]
        for j in range(c):
            size = (j + 1) * W
            part = dot3_nt((row[0][:, :size], row[1][:, :size]), halves[j])
            parts.append(split(part))
            block = block - dot3_nt(parts[j], parts[j])
    work[...] = block
    eliminate(work)
    if not last:
        own = jnp.where(lane <= sub, work[...], 0.0)
        out_ref[:, c * W :] = own
    else:
        count = out_ref.shape[1]
        start = pl.multiple_of(member * count, 8)
        own_lane = lax.broadcasted_iota(jnp.int32, (count, W), 1)
        own_row = lax.broadcasted_iota(jnp.int32, (count, W), 0) + start
        own = jnp.where(own_lane <= own_row, work[pl.ds(start, count), :], 0.0)

    def left_of_own():
        own_halves = split(own)
        sums = [None] * c
        for j in range(c):
            ahead = split(dot3(own_halves, parts[j]))
            for i in range(j + 1):
                at = slice(i * W, (i + 1) * W)
                term = dot3(ahead, (halves[j][0][:, at], halves[j][1][:, at]))
                sums[i] = term if sums[i] is None else sums[i] + term
        return sums

    if not last:
        if c:
            for i, total in enumerate(left_of_own()):
                out_ref[:, i * W : (i + 1) * W] = -total
        return

    for j in range(c):

        @pl.when(slab == j)
        def _():
            size = (j + 1) * W
            out_ref[0, :, :size] = before[j][pl.ds(start, count), :]
            out_ref[0, :, size:] = jnp.zeros((count, BLK - size), f32)

    @pl.when(slab == c)
    def _():
        for i, total in enumerate(left_of_own()):
            out_ref[0, :, i * W : (i + 1) * W] = -total
        out_ref[0, :, c * W :] = own


def factor(c, first, shares, before, tokens, members):
    last = c == CHUNKS - 1
    shape = (1, W // members, BLK) if last else (W, (c + 1) * W)
    vmem = pl.BlockSpec(memory_space=pltpu.VMEM)
    return pl.pallas_call(
        lambda *refs: factor_body(c, first, tokens, members, *refs),
        out_shape=jax.ShapeDtypeStruct(shape, f32),
        in_specs=[vmem] * (CHUNKS + c),
        out_specs=vmem,
        scratch_shapes=[pltpu.VMEM((W, W), f32), pltpu.VMEM((W, (c + 1) * W), f32)],
        compiler_params=pltpu.CompilerParams(vmem_limit_bytes=VMEM),
        cost_estimate=pl.CostEstimate(
            flops=100_000_000 if c in EARLY else 20_000_000_000,
            bytes_accessed=8 * W * W * (c + 1),
            transcendentals=0,
        ),
    )(*shares, *before)


def on_device(embedded, out_grads, section_gains, plan):
    data_count = lax.axis_size("dp")
    micro, rows, _ = embedded.shape
    slab = data_count // CHUNKS
    along = [[z + slab * x for z in range(slab)] for x in range(CHUNKS)]
    gains = lax.all_gather(section_gains, "pipe", axis=0)
    normed, left, right = relay(plan, embedded, gains, out_grads)

    def along_slab(tiles, steps):
        pairs = [
            (z + slab * x, (z + steps) % slab + slab * x)
            for x in range(CHUNKS)
            for z in range(slab)
        ]
        return lax.ppermute(tiles, "dp", pairs)

    def from_slabs(tiles):
        shares = [tiles]
        for steps in range(1, CHUNKS):
            pairs = [
                (z + slab * x, z + slab * ((x + steps) % CHUNKS))
                for z in range(slab)
                for x in range(CHUNKS)
            ]
            shares.append(lax.ppermute(tiles, "dp", pairs))
        return shares

    lefts = from_slabs(left)
    right, *early = covariance(EARLY, lefts, [right], slab)
    rights = from_slabs(right)
    (late,) = covariance(LATE, lefts, rights, slab)
    early = fold(early[:1] + [along_slab(early[k], k) for k in range(1, slab)], late)
    early = lay([early] + [along_slab(early, k) for k in range(1, slab)]).reshape(-1, 8, B)
    late = lax.psum(late, "dp", axis_index_groups=along)

    tokens = micro * rows * data_count
    before = []
    shares = from_slabs(early)
    for c in EARLY:
        before.append(factor(c, tile_count(range(c)), shares, before, tokens, slab))
    after = before[-1:]
    for c in LATE:
        shares = from_slabs(later(late, c, after))
        after = shares[1:]
        before.append(factor(c, 0, shares, before, tokens, slab))
    return normed, before[-1]


def solution(mesh):
    in_specs = (P(None, "dp", None), P("pipe", None, "dp", None), P("pipe", None), P())
    out_specs = (P("pipe", None, "dp", None), P("pipe", "dp", None))
    return jax.shard_map(
        on_device, mesh=mesh, in_specs=in_specs, out_specs=out_specs, check_vma=False
    )
```

```python
import jax
import jax.numpy as jnp
from jax import lax
from jax.experimental import pallas as pl
from jax.experimental.pallas import tpu as pltpu
from jax.sharding import PartitionSpec as P

BLK = 1536
B = 128
CHUNKS = 4
W = BLK // CHUNKS
EARLY, LATE = (0, 1, 2), (3,)
LEFT = len(EARLY) * W
RIGHT = BLK - LEFT
DAMPING = 0.1
EPS = 1e-5
VMEM = 40 * 2**20
SPAN = 512

f32 = jnp.float32
bf16 = jnp.bfloat16


def split(x):
    high = x.astype(bf16)
    low = (x - high.astype(f32)).astype(bf16)
    return high, low


def dot(a, b):
    return jnp.dot(a, b, preferred_element_type=f32)


def dot3(a, b):
    return dot(a[0], b[0]) + dot(a[1], b[0]) + dot(a[0], b[1])


def dot3_nt(a, b):
    def one(x, y):
        return lax.dot_general(x, y, (((1,), (1,)), ((), ())), preferred_element_type=f32)

    return one(a[0], b[0]) + one(a[1], b[0]) + one(a[0], b[1])


def relay_body(
    plan, embedded_ref, gains_ref, grads_ref, normed_ref, left_ref, right_ref, hidden_ref
):
    section = lax.axis_index("pipe")
    block_id = plan[section, 0]
    rows, width = hidden_ref.shape
    spans = [(start, SPAN) for start in range(0, width, SPAN)]

    def squares(total, h):
        square = h * h
        for lane in range(0, SPAN, 128):
            total = total + square[:, lane : lane + 128]
        return total

    def scale_of(total):
        mean = jnp.sum(total, axis=1, keepdims=True) * (1.0 / width)
        return jnp.broadcast_to(lax.rsqrt(mean + EPS), (rows, SPAN))

    total = jnp.zeros((rows, 128), f32)
    for start, size in spans:
        h = embedded_ref[0, :, start : start + size].astype(f32)
        hidden_ref[:, start : start + size] = h
        total = squares(total, h)

    def one_section(s, total):
        scale = scale_of(total)
        total = jnp.zeros((rows, 128), f32)
        for start, size in spans:
            h = hidden_ref[:, start : start + size]
            gain = gains_ref[s, :, start : start + size]
            half = h * scale * (gain * 0.5)
            h = h + (half + half * jnp.tanh(half))
            hidden_ref[:, start : start + size] = h
            total = squares(total, h)
        return total

    total = lax.fori_loop(0, section, one_section, total)
    scale = scale_of(total)
    for start, size in spans:
        h = hidden_ref[:, start : start + size]
        gain = gains_ref[section, :, start : start + size]
        normed_ref[0, 0, :, start : start + size] = h * scale * gain

    for first, size, ref in ((0, LEFT, left_ref), (LEFT, RIGHT, right_ref)):

        @pl.when(block_id < width // BLK)
        def _():
            place = pl.multiple_of(block_id * BLK + first, W)
            ref[...] = normed_ref[0, 0, :, pl.ds(place, size)]

        @pl.when(block_id >= width // BLK)
        def _():
            ref[...] = grads_ref[0, 0, :, first : first + size].astype(f32)


def relay(plan, embedded, gains, grads):
    micro, rows, width = embedded.shape
    sections = gains.shape[0]
    blocks = width // BLK

    def grads_block(m, plan):
        return 0, m, 0, jnp.maximum(plan[lax.axis_index("pipe"), 0] - blocks, 0)

    return pl.pallas_call(
        relay_body,
        grid_spec=pltpu.PrefetchScalarGridSpec(
            num_scalar_prefetch=1,
            grid=(micro,),
            in_specs=[
                pl.BlockSpec((1, rows, width), lambda m, plan: (m, 0, 0)),
                pl.BlockSpec((sections, 1, width), lambda m, plan: (0, 0, 0)),
                pl.BlockSpec((1, 1, rows, BLK), grads_block),
            ],
            out_specs=[
                pl.BlockSpec((1, 1, rows, width), lambda m, plan: (0, m, 0, 0)),
                pl.BlockSpec((rows, LEFT), lambda m, plan: (m, 0)),
                pl.BlockSpec((rows, RIGHT), lambda m, plan: (m, 0)),
            ],
            scratch_shapes=[pltpu.VMEM((rows, width), f32)],
        ),
        out_shape=[
            jax.ShapeDtypeStruct((1, micro, rows, width), f32),
            jax.ShapeDtypeStruct((micro * rows, LEFT), f32),
            jax.ShapeDtypeStruct((micro * rows, RIGHT), f32),
        ],
        compiler_params=pltpu.CompilerParams(vmem_limit_bytes=VMEM),
    )(plan, embedded, gains, grads)


def tiles_of(c):
    for block in range(W // B):
        for group in range(B // 8 // CHUNKS):
            for tile in range(c * W // B + block + 1):
                yield block, group, tile


def tile_count(chunks):
    return sum(len(list(tiles_of(c))) for c in chunks)


def tiles_each(chunks, members):
    return -(-tile_count(chunks) // members)


def slab_member(members):
    index = lax.axis_index("dp")
    return lax.div(index, members), lax.rem(index, members)


def covariance_body(members, *refs):
    left_refs, right_ref, copy_ref = refs[:CHUNKS], refs[CHUNKS], refs[CHUNKS + 1]
    *out_refs, tiles_ref, turned = refs[CHUNKS + 2 :]
    copy_ref[...] = right_ref[...]
    columns = jnp.concatenate([ref[...] for ref in left_refs], 0)
    turned[...] = columns.T.reshape(turned.shape)
    slab, member = slab_member(members)
    left = turned[:, slab]
    groups, eight, tokens = left.shape
    left = left.reshape(groups * eight, tokens).astype(bf16)
    product = dot(left, columns.astype(bf16))
    per_block = B // 8 // CHUNKS
    index = 0
    for c in EARLY:
        for block, group, tile in tiles_of(c):
            row = 8 * ((c * (W // B) + block) * per_block + group)
            tiles_ref[index] = product[row : row + 8, tile * B : (tile + 1) * B]
            index += 1
    each = out_refs[0].shape[0]
    tiles_ref[index:] = jnp.zeros((each * members - index, 8, B), f32)
    for steps, ref in enumerate(out_refs):
        first = lax.rem(member + steps, members) * each
        ref[...] = tiles_ref[pl.ds(first, each)]


def covariance(lefts, right, members):
    tokens = len(lefts) * lefts[0].shape[0]
    vmem = pl.BlockSpec(memory_space=pltpu.VMEM)
    each = tiles_each(EARLY, members)
    out_shape = [jax.ShapeDtypeStruct(right.shape, f32)]
    out_shape += [jax.ShapeDtypeStruct((each, 8, B), f32)] * members
    return pl.pallas_call(
        lambda *refs: covariance_body(members, *refs),
        out_shape=out_shape,
        in_specs=[vmem] * (len(lefts) + 1),
        out_specs=[vmem] * len(out_shape),
        scratch_shapes=[
            pltpu.VMEM((each * members, 8, B), f32),
            pltpu.VMEM((LEFT // 8 // CHUNKS, CHUNKS, 8, tokens), f32),
        ],
        compiler_params=pltpu.CompilerParams(vmem_limit_bytes=VMEM),
    )(*lefts, right)


def late_covariance_body(*refs):
    *column_refs, out_ref = refs
    left, right = (
        jnp.concatenate([ref[...].astype(bf16) for ref in part], 0)
        for part in (column_refs[:CHUNKS], column_refs[CHUNKS:])
    )
    turned = jnp.concatenate([ref[...] for ref in column_refs[CHUNKS:]], 0).T.astype(bf16)
    first = 0
    for place, c in enumerate(LATE):
        rows = turned[place * W : (place + 1) * W]
        size = (c + 1) * W
        out_ref[:, first : first + LEFT] = dot(rows, left)
        out_ref[:, first + LEFT : first + size] = dot(rows, right[:, : size - LEFT])
        first += size


def late_covariance(lefts, rights):
    vmem = pl.BlockSpec(memory_space=pltpu.VMEM)
    return pl.pallas_call(
        late_covariance_body,
        out_shape=jax.ShapeDtypeStruct((W, sum(c + 1 for c in LATE) * W), f32),
        in_specs=[vmem] * (len(lefts) + len(rights)),
        out_specs=vmem,
        compiler_params=pltpu.CompilerParams(vmem_limit_bytes=VMEM),
    )(*lefts, *rights)


def fold_body(count, *refs):
    part_refs, out_ref = refs[:count], refs[-1]
    total = part_refs[0][...]
    for ref in part_refs[1:]:
        total = total + ref[...]
    out_ref[...] = total


def fold(parts, *after):
    vmem = pl.BlockSpec(memory_space=pltpu.VMEM)
    return pl.pallas_call(
        lambda *refs: fold_body(len(parts), *refs),
        out_shape=jax.ShapeDtypeStruct(parts[0].shape, f32),
        in_specs=[vmem] * len(parts) + [pl.BlockSpec(memory_space=pl.ANY)] * len(after),
        out_specs=vmem,
    )(*parts, *after)


def lay_body(members, *refs):
    part_refs, first_ref, last_ref, tiles_ref = refs[:members], *refs[members:]
    _, member = slab_member(members)
    each = part_refs[0].shape[0]
    for steps, ref in enumerate(part_refs):
        first = lax.rem(member + (members - steps), members) * each
        tiles_ref[pl.ds(first, each)] = ref[...]
    split_at = first_ref.shape[0]
    first_ref[...] = tiles_ref[:split_at]
    last_ref[...] = tiles_ref[split_at : split_at + last_ref.shape[0]]


def lay(parts):
    members = len(parts)
    vmem = pl.BlockSpec(memory_space=pltpu.VMEM)
    return pl.pallas_call(
        lambda *refs: lay_body(members, *refs),
        out_shape=[
            jax.ShapeDtypeStruct((tile_count(chunks), 8, B), f32)
            for chunks in (EARLY[:-1], EARLY[-1:])
        ],
        in_specs=[vmem] * members,
        out_specs=[vmem] * 2,
        scratch_shapes=[pltpu.VMEM((members * parts[0].shape[0], 8, B), f32)],
    )(*parts)


def later_body(tiles_ref, *refs):
    refs[-1][...] = tiles_ref[...]


def later(tiles, after):
    vmem = pl.BlockSpec(memory_space=pltpu.VMEM)
    return pl.pallas_call(
        later_body,
        out_shape=jax.ShapeDtypeStruct(tiles.shape, f32),
        in_specs=[vmem] + [pl.BlockSpec(memory_space=pl.ANY)] * len(after),
        out_specs=vmem,
    )(tiles, *after)


def across_rows(x, j):
    return jnp.broadcast_to(x[j : j + 1, :], x.shape)


def across_lanes(x, j):
    return jnp.broadcast_to(x[:, j : j + 1], x.shape)


def reciprocal(p):
    r = pl.reciprocal(p, approx=True)
    return r * (2.0 - p * r)


def inverse_factor(d):
    sub = lax.broadcasted_iota(jnp.int32, (8, 128), 0)
    lane = lax.broadcasted_iota(jnp.int32, (8, 128), 1)
    rows = [d[8 * i : 8 * i + 8, :] for i in range(16)]
    for t in range(8):
        pair = [rows[2 * t], rows[2 * t + 1]]
        cols = [[across_lanes(x, 16 * t + j) for j in range(16)] for x in pair]
        own = (lane >= 16 * t) & (lane < 16 * t + 16)
        for half in range(2):
            one = (lane - 16 * t - 8 * half == sub).astype(f32)
            pair[half] = jnp.where(own, one, pair[half])
        scales = []
        for half in range(2):
            pivots = jnp.zeros((8, 128), f32)
            mine = cols[half]
            for i in range(0, 8, 2):
                j = 8 * half + i
                x, y = mine[j], mine[j + 1]
                a, b, c = across_rows(x, i), across_rows(y, i), across_rows(y, i + 1)
                det = a * c - b * b
                r = pl.reciprocal(det, approx=True)
                fix = 2.0 - det * r
                ra = reciprocal(a)
                pivots = jnp.where(sub == i, a, jnp.where(sub == i + 1, det * ra, pivots))
                within = jnp.where(sub == i + 1, b * ra, 0.0)
                first, second = across_rows(pair[half], i), across_rows(pair[half], i + 1)
                if i < 6:
                    below = sub > i + 1
                    m0 = jnp.where(below, (x * c - y * b) * r, 0.0) * fix
                    m1 = jnp.where(below, (y * a - x * b) * r, 0.0) * fix
                if half == 0:
                    x, y = cols[1][j], cols[1][j + 1]
                    n0 = (x * c - y * b) * r * fix
                    n1 = (y * a - x * b) * r * fix
                for q in range(j + 2, 16):
                    s0, s1 = across_rows(mine[q], i), across_rows(mine[q], i + 1)
                    if i < 6:
                        mine[q] = mine[q] - (m0 * s0 + m1 * s1)
                    if half == 0:
                        cols[1][q] = cols[1][q] - (n0 * s0 + n1 * s1)
                if i < 6:
                    pair[half] = pair[half] - ((m0 + within) * first + m1 * second)
                else:
                    pair[half] = pair[half] - within * first
                if half == 0:
                    pair[1] = pair[1] - (n0 * first + n1 * second)
            scales.append(lax.rsqrt(pivots))
        done = [pair[half] * scales[half] for half in range(2)]
        rows[2 * t], rows[2 * t + 1] = done
        if t < 7:
            left = split(jnp.concatenate(pair, 0))
            right = split(jnp.concatenate([done[half] * scales[half] for half in range(2)], 0))
            update = lax.dot_general(
                jnp.concatenate([left[0], left[0], left[1]], 0),
                jnp.concatenate([right[0], right[1], right[0]], 0),
                (((0,), (0,)), ((), ())),
                preferred_element_type=f32,
            )
            for i in range(2 * t + 2, 16):
                rows[i] = jnp.where(own, 0.0, rows[i]) - update[8 * i : 8 * i + 8, :]
    return jnp.concatenate(rows, 0)


def eliminate(work):
    size = work.shape[0]
    lane = lax.broadcasted_iota(jnp.int32, (B, B), 1)
    sub = lax.broadcasted_iota(jnp.int32, (B, B), 0)
    for done in range(0, size, B):
        rows = slice(done, done + B)
        w = jnp.where(lane <= sub, inverse_factor(work[rows, rows]), 0.0)
        new = dot3(split(w), split(work[rows, :]))
        work[rows, :] = new
        work[rows, rows] = w
        if done + B == size:
            break
        turned_high, turned_low = split(work[rows, done + B :].T)
        high, low = split(work[rows, :])
        for start in range(done + B, size, B):
            at = slice(start - done - B, start - done)
            left = (turned_high[at], turned_low[at])
            target = slice(start, start + B)
            x = dot3(left, (high[:, : done + B], low[:, : done + B]))
            if done:
                work[target, :done] = work[target, :done] - x[:, :done]
            work[target, rows] = -x[:, done:]
            y = dot3(left, (high[:, start:], low[:, start:]))
            work[target, start:] = work[target, start:] - y


def factor_body(c, tokens, members, *refs):
    last = c == CHUNKS - 1
    slab, member = slab_member(members)
    if c in EARLY:
        share_refs = refs[:CHUNKS]
        *before, out_ref, work, rows_ref = refs[CHUNKS:]
        first = 0 if c == EARLY[-1] else tile_count(range(c))
        for steps, ref in enumerate(share_refs):
            x = lax.rem(slab + (CHUNKS - steps), CHUNKS)
            for index, (block, group, tile) in enumerate(tiles_of(c)):
                row = pl.multiple_of(8 * x + (block * B + 8 * CHUNKS * group), 8)
                rows_ref[pl.ds(row, 8), tile * B : (tile + 1) * B] = ref[first + index]
        for block in range(W // B):
            for other in range(block):
                rows = slice(block * B, (block + 1) * B)
                at = c * W + other * B
                low = rows_ref[rows, at : at + B]
                rows_ref[other * B : (other + 1) * B, c * W + block * B : c * W + (block + 1) * B] = low.T
    else:
        late_ref, *before, out_ref, work, rows_ref, semaphore = refs
        first = sum(late + 1 for late in LATE if late < c) * W
        copy = pltpu.make_async_copy(
            late_ref.at[:, first : first + (c + 1) * W], rows_ref, semaphore
        )
        copy.start()
        copy.wait()
    lane = lax.broadcasted_iota(jnp.int32, (W, W), 1)
    sub = lax.broadcasted_iota(jnp.int32, (W, W), 0)
    scale = 1.0 / tokens
    block = rows_ref[:, c * W :] * scale + jnp.where(lane == sub, DAMPING, 0.0)
    parts = []
    if c:
        row = split(rows_ref[:, : c * W] * scale)
        halves = [split(ref[...]) for ref in before]
        for j in range(c):
            size = (j + 1) * W
            part = dot3_nt((row[0][:, :size], row[1][:, :size]), halves[j])
            parts.append(split(part))
            block = block - dot3_nt(parts[j], parts[j])
    work[...] = block
    eliminate(work)
    if not last:
        own = jnp.where(lane <= sub, work[...], 0.0)
        out_ref[:, c * W :] = own
    else:
        count = out_ref.shape[1]
        start = pl.multiple_of(member * count, 8)
        own_lane = lax.broadcasted_iota(jnp.int32, (count, W), 1)
        own_row = lax.broadcasted_iota(jnp.int32, (count, W), 0) + start
        own = jnp.where(own_lane <= own_row, work[pl.ds(start, count), :], 0.0)

    def left_of_own():
        own_halves = split(own)
        sums = [None] * c
        for j in range(c):
            ahead = split(dot3(own_halves, parts[j]))
            for i in range(j + 1):
                at = slice(i * W, (i + 1) * W)
                term = dot3(ahead, (halves[j][0][:, at], halves[j][1][:, at]))
                sums[i] = term if sums[i] is None else sums[i] + term
        return sums

    if not last:
        if c:
            for i, total in enumerate(left_of_own()):
                out_ref[:, i * W : (i + 1) * W] = -total
        return

    for j in range(c):

        @pl.when(slab == j)
        def _():
            size = (j + 1) * W
            out_ref[0, :, :size] = before[j][pl.ds(start, count), :]
            out_ref[0, :, size:] = jnp.zeros((count, BLK - size), f32)

    @pl.when(slab == c)
    def _():
        for i, total in enumerate(left_of_own()):
            out_ref[0, :, i * W : (i + 1) * W] = -total
        out_ref[0, :, c * W :] = own


def factor(c, shares, before, tokens, members):
    shape = (1, W // members, BLK) if c == CHUNKS - 1 else (W, (c + 1) * W)
    vmem = pl.BlockSpec(memory_space=pltpu.VMEM)
    scratch = [pltpu.VMEM((W, W), f32), pltpu.VMEM((W, (c + 1) * W), f32)]
    if c in EARLY:
        in_specs = [vmem] * len(shares)
    else:
        in_specs = [pl.BlockSpec(memory_space=pl.ANY)]
        scratch.append(pltpu.SemaphoreType.DMA)
    return pl.pallas_call(
        lambda *refs: factor_body(c, tokens, members, *refs),
        out_shape=jax.ShapeDtypeStruct(shape, f32),
        in_specs=in_specs + [vmem] * c,
        out_specs=vmem,
        scratch_shapes=scratch,
        compiler_params=pltpu.CompilerParams(vmem_limit_bytes=VMEM),
        cost_estimate=pl.CostEstimate(
            flops=10_000_000_000 if c == 1 else 100_000_000,
            bytes_accessed=8 * W * W * (c + 1),
            transcendentals=0,
        ),
    )(*shares, *before)


def on_device(embedded, out_grads, section_gains, plan):
    data_count = lax.axis_size("dp")
    micro, rows, _ = embedded.shape
    slab = data_count // CHUNKS
    along = [[z + slab * x for z in range(slab)] for x in range(CHUNKS)]
    gains = lax.all_gather(section_gains, "pipe", axis=0)
    normed, left, right = relay(plan, embedded, gains, out_grads)

    def along_slab(tiles, steps):
        pairs = [
            (z + slab * x, (z + steps) % slab + slab * x)
            for x in range(CHUNKS)
            for z in range(slab)
        ]
        return lax.ppermute(tiles, "dp", pairs)

    def from_slabs(tiles):
        shares = [tiles]
        for steps in range(1, CHUNKS):
            pairs = [
                (z + slab * x, z + slab * ((x + steps) % CHUNKS))
                for z in range(slab)
                for x in range(CHUNKS)
            ]
            shares.append(lax.ppermute(tiles, "dp", pairs))
        return shares

    lefts = from_slabs(left)
    right, *early = covariance(lefts, right, slab)
    rights = from_slabs(right)
    late = late_covariance(lefts, rights)
    early = fold(early[:1] + [along_slab(early[k], k) for k in range(1, slab)], late)
    early, middle = lay([early] + [along_slab(early, k) for k in range(1, slab)])
    late = lax.psum(late, "dp", axis_index_groups=along)

    tokens = micro * rows * data_count
    early = from_slabs(early)
    middle = from_slabs(later(middle, early[1:]))
    before = []
    for c, shares in zip(range(CHUNKS), (early, early, middle, [late])):
        before.append(factor(c, shares, before, tokens, slab))
    return normed, before[-1]


def solution(mesh):
    in_specs = (P(None, "dp", None), P("pipe", None, "dp", None), P("pipe", None), P())
    out_specs = (P("pipe", None, "dp", None), P("pipe", "dp", None))
    return jax.shard_map(
        on_device, mesh=mesh, in_specs=in_specs, out_specs=out_specs, check_vma=False
    )
```

```python
import jax
import jax.numpy as jnp
from jax import lax
from jax.experimental import pallas as pl
from jax.experimental.pallas import tpu as pltpu
from jax.sharding import PartitionSpec as P

BLK = 1536
B = 128
CHUNKS = 4
W = BLK // CHUNKS
EARLY, LATE = (0, 1, 2), (3,)
LEFT = len(EARLY) * W
RIGHT = BLK - LEFT
DAMPING = 0.1
EPS = 1e-5
VMEM = 40 * 2**20
SPAN = 512

f32 = jnp.float32
bf16 = jnp.bfloat16


def split(x):
    high = x.astype(bf16)
    low = (x - high.astype(f32)).astype(bf16)
    return high, low


def dot(a, b):
    return jnp.dot(a, b, preferred_element_type=f32)


def dot3(a, b):
    return dot(a[0], b[0]) + dot(a[1], b[0]) + dot(a[0], b[1])


def dot3_nt(a, b):
    def one(x, y):
        return lax.dot_general(x, y, (((1,), (1,)), ((), ())), preferred_element_type=f32)

    return one(a[0], b[0]) + one(a[1], b[0]) + one(a[0], b[1])


def relay_body(
    plan, embedded_ref, gains_ref, grads_ref, normed_ref, left_ref, right_ref, hidden_ref
):
    section = lax.axis_index("pipe")
    block_id = plan[section, 0]
    rows, width = hidden_ref.shape
    spans = [(start, SPAN) for start in range(0, width, SPAN)]

    def squares(total, h):
        square = h * h
        for lane in range(0, SPAN, 128):
            total = total + square[:, lane : lane + 128]
        return total

    def scale_of(total):
        mean = jnp.sum(total, axis=1, keepdims=True) * (1.0 / width)
        return jnp.broadcast_to(lax.rsqrt(mean + EPS), (rows, SPAN))

    total = jnp.zeros((rows, 128), f32)
    for start, size in spans:
        h = embedded_ref[0, :, start : start + size].astype(f32)
        hidden_ref[:, start : start + size] = h
        total = squares(total, h)

    def one_section(s, total):
        scale = scale_of(total)
        total = jnp.zeros((rows, 128), f32)
        for start, size in spans:
            h = hidden_ref[:, start : start + size]
            gain = gains_ref[s, :, start : start + size]
            half = h * scale * (gain * 0.5)
            h = h + (half + half * jnp.tanh(half))
            hidden_ref[:, start : start + size] = h
            total = squares(total, h)
        return total

    total = lax.fori_loop(0, section, one_section, total)
    scale = scale_of(total)
    for start, size in spans:
        h = hidden_ref[:, start : start + size]
        gain = gains_ref[section, :, start : start + size]
        normed_ref[0, 0, :, start : start + size] = h * scale * gain

    for first, size, ref in ((0, LEFT, left_ref), (LEFT, RIGHT, right_ref)):

        @pl.when(block_id < width // BLK)
        def _():
            place = pl.multiple_of(block_id * BLK + first, W)
            ref[...] = normed_ref[0, 0, :, pl.ds(place, size)]

        @pl.when(block_id >= width // BLK)
        def _():
            ref[...] = grads_ref[0, 0, :, first : first + size].astype(f32)


def relay(plan, embedded, gains, grads):
    micro, rows, width = embedded.shape
    sections = gains.shape[0]
    blocks = width // BLK

    def grads_block(m, plan):
        return 0, m, 0, jnp.maximum(plan[lax.axis_index("pipe"), 0] - blocks, 0)

    return pl.pallas_call(
        relay_body,
        grid_spec=pltpu.PrefetchScalarGridSpec(
            num_scalar_prefetch=1,
            grid=(micro,),
            in_specs=[
                pl.BlockSpec((1, rows, width), lambda m, plan: (m, 0, 0)),
                pl.BlockSpec((sections, 1, width), lambda m, plan: (0, 0, 0)),
                pl.BlockSpec((1, 1, rows, BLK), grads_block),
            ],
            out_specs=[
                pl.BlockSpec((1, 1, rows, width), lambda m, plan: (0, m, 0, 0)),
                pl.BlockSpec((rows, LEFT), lambda m, plan: (m, 0)),
                pl.BlockSpec((rows, RIGHT), lambda m, plan: (m, 0)),
            ],
            scratch_shapes=[pltpu.VMEM((rows, width), f32)],
        ),
        out_shape=[
            jax.ShapeDtypeStruct((1, micro, rows, width), f32),
            jax.ShapeDtypeStruct((micro * rows, LEFT), f32),
            jax.ShapeDtypeStruct((micro * rows, RIGHT), f32),
        ],
        compiler_params=pltpu.CompilerParams(vmem_limit_bytes=VMEM),
    )(plan, embedded, gains, grads)


def tiles_of(c):
    for block in range(W // B):
        for group in range(B // 8 // CHUNKS):
            for tile in range(c * W // B + block + 1):
                yield block, group, tile


def tile_count(chunks):
    return sum(len(list(tiles_of(c))) for c in chunks)


def tiles_each(chunks, members):
    return -(-tile_count(chunks) // members)


def slab_member(members):
    index = lax.axis_index("dp")
    return lax.div(index, members), lax.rem(index, members)


def covariance_body(members, *refs):
    left_refs, right_ref, copy_ref = refs[:CHUNKS], refs[CHUNKS], refs[CHUNKS + 1]
    out_ref, turned = refs[CHUNKS + 2 :]
    copy_ref[...] = right_ref[...]
    columns = jnp.concatenate([ref[...] for ref in left_refs], 0)
    turned[...] = columns.T.reshape(turned.shape)
    slab, _ = slab_member(members)
    left = turned[:, slab]
    groups, eight, tokens = left.shape
    left = left.reshape(groups * eight, tokens).astype(bf16)
    product = dot(left, columns.astype(bf16))
    per_block = B // 8 // CHUNKS
    each = out_ref.shape[1]
    index = 0
    for c in EARLY:
        for block, group, tile in tiles_of(c):
            row = 8 * ((c * (W // B) + block) * per_block + group)
            out_ref[index // each, index % each] = product[
                row : row + 8, tile * B : (tile + 1) * B
            ]
            index += 1
    while index < each * members:
        out_ref[index // each, index % each] = jnp.zeros((8, B), f32)
        index += 1


def covariance(lefts, right, members):
    tokens = len(lefts) * lefts[0].shape[0]
    vmem = pl.BlockSpec(memory_space=pltpu.VMEM)
    each = tiles_each(EARLY, members)
    out_shape = [jax.ShapeDtypeStruct(right.shape, f32)]
    out_shape.append(jax.ShapeDtypeStruct((members, each, 8, B), f32))
    return pl.pallas_call(
        lambda *refs: covariance_body(members, *refs),
        out_shape=out_shape,
        in_specs=[vmem] * (len(lefts) + 1),
        out_specs=[vmem] * len(out_shape),
        scratch_shapes=[
            pltpu.VMEM((LEFT // 8 // CHUNKS, CHUNKS, 8, tokens), f32),
        ],
        compiler_params=pltpu.CompilerParams(vmem_limit_bytes=VMEM),
    )(*lefts, right)


def late_covariance_body(*refs):
    *column_refs, out_ref = refs
    left, right = (
        jnp.concatenate([ref[...].astype(bf16) for ref in part], 0)
        for part in (column_refs[:CHUNKS], column_refs[CHUNKS:])
    )
    turned = jnp.concatenate([ref[...] for ref in column_refs[CHUNKS:]], 0).T.astype(bf16)
    first = 0
    for place, c in enumerate(LATE):
        rows = turned[place * W : (place + 1) * W]
        size = (c + 1) * W
        out_ref[:, first : first + LEFT] = dot(rows, left)
        out_ref[:, first + LEFT : first + size] = dot(rows, right[:, : size - LEFT])
        first += size


def late_covariance(lefts, rights):
    vmem = pl.BlockSpec(memory_space=pltpu.VMEM)
    return pl.pallas_call(
        late_covariance_body,
        out_shape=jax.ShapeDtypeStruct((W, sum(c + 1 for c in LATE) * W), f32),
        in_specs=[vmem] * (len(lefts) + len(rights)),
        out_specs=vmem,
        compiler_params=pltpu.CompilerParams(vmem_limit_bytes=VMEM),
    )(*lefts, *rights)


def fold_body(parts_ref, *refs):
    total = parts_ref[0]
    for member in range(1, parts_ref.shape[0]):
        total = total + parts_ref[member]
    refs[-1][...] = total


def fold(parts, *after):
    vmem = pl.BlockSpec(memory_space=pltpu.VMEM)
    return pl.pallas_call(
        fold_body,
        out_shape=jax.ShapeDtypeStruct(parts.shape[1:], f32),
        in_specs=[vmem] + [pl.BlockSpec(memory_space=pl.ANY)] * len(after),
        out_specs=vmem,
    )(parts, *after)


def lay_body(members, *refs):
    part_refs, first_ref, last_ref, tiles_ref = refs[:members], *refs[members:]
    _, member = slab_member(members)
    each = part_refs[0].shape[0]
    for steps, ref in enumerate(part_refs):
        first = lax.rem(member + (members - steps), members) * each
        tiles_ref[pl.ds(first, each)] = ref[...]
    split_at = first_ref.shape[0]
    first_ref[...] = tiles_ref[:split_at]
    last_ref[...] = tiles_ref[split_at : split_at + last_ref.shape[0]]


def lay(parts):
    members = len(parts)
    vmem = pl.BlockSpec(memory_space=pltpu.VMEM)
    return pl.pallas_call(
        lambda *refs: lay_body(members, *refs),
        out_shape=[
            jax.ShapeDtypeStruct((tile_count(chunks), 8, B), f32)
            for chunks in (EARLY[:-1], EARLY[-1:])
        ],
        in_specs=[vmem] * members,
        out_specs=[vmem] * 2,
        scratch_shapes=[pltpu.VMEM((members * parts[0].shape[0], 8, B), f32)],
    )(*parts)


def later_body(tiles_ref, *refs):
    refs[-1][...] = tiles_ref[...]


def later(tiles, after):
    vmem = pl.BlockSpec(memory_space=pltpu.VMEM)
    return pl.pallas_call(
        later_body,
        out_shape=jax.ShapeDtypeStruct(tiles.shape, f32),
        in_specs=[vmem] + [pl.BlockSpec(memory_space=pl.ANY)] * len(after),
        out_specs=vmem,
    )(tiles, *after)


def across_rows(x, j):
    return jnp.broadcast_to(x[j : j + 1, :], x.shape)


def across_lanes(x, j):
    return jnp.broadcast_to(x[:, j : j + 1], x.shape)


def reciprocal(p):
    r = pl.reciprocal(p, approx=True)
    return r * (2.0 - p * r)


def inverse_factor(d):
    sub = lax.broadcasted_iota(jnp.int32, (8, 128), 0)
    lane = lax.broadcasted_iota(jnp.int32, (8, 128), 1)
    rows = [d[8 * i : 8 * i + 8, :] for i in range(16)]
    for t in range(8):
        pair = [rows[2 * t], rows[2 * t + 1]]
        cols = [[across_lanes(x, 16 * t + j) for j in range(16)] for x in pair]
        own = (lane >= 16 * t) & (lane < 16 * t + 16)
        for half in range(2):
            one = (lane - 16 * t - 8 * half == sub).astype(f32)
            pair[half] = jnp.where(own, one, pair[half])
        scales = []
        for half in range(2):
            pivots = jnp.zeros((8, 128), f32)
            mine = cols[half]
            for i in range(0, 8, 2):
                j = 8 * half + i
                x, y = mine[j], mine[j + 1]
                a, b, c = across_rows(x, i), across_rows(y, i), across_rows(y, i + 1)
                det = a * c - b * b
                r = pl.reciprocal(det, approx=True)
                fix = 2.0 - det * r
                ra = reciprocal(a)
                pivots = jnp.where(sub == i, a, jnp.where(sub == i + 1, det * ra, pivots))
                within = jnp.where(sub == i + 1, b * ra, 0.0)
                first, second = across_rows(pair[half], i), across_rows(pair[half], i + 1)
                if i < 6:
                    below = sub > i + 1
                    m0 = jnp.where(below, (x * c - y * b) * r, 0.0) * fix
                    m1 = jnp.where(below, (y * a - x * b) * r, 0.0) * fix
                if half == 0:
                    x, y = cols[1][j], cols[1][j + 1]
                    n0 = (x * c - y * b) * r * fix
                    n1 = (y * a - x * b) * r * fix
                for q in range(j + 2, 16):
                    s0, s1 = across_rows(mine[q], i), across_rows(mine[q], i + 1)
                    if i < 6:
                        mine[q] = mine[q] - (m0 * s0 + m1 * s1)
                    if half == 0:
                        cols[1][q] = cols[1][q] - (n0 * s0 + n1 * s1)
                if i < 6:
                    pair[half] = pair[half] - ((m0 + within) * first + m1 * second)
                else:
                    pair[half] = pair[half] - within * first
                if half == 0:
                    pair[1] = pair[1] - (n0 * first + n1 * second)
            scales.append(lax.rsqrt(pivots))
        done = [pair[half] * scales[half] for half in range(2)]
        rows[2 * t], rows[2 * t + 1] = done
        if t < 7:
            left = split(jnp.concatenate(pair, 0))
            right = split(jnp.concatenate([done[half] * scales[half] for half in range(2)], 0))
            update = lax.dot_general(
                jnp.concatenate([left[0], left[0], left[1]], 0),
                jnp.concatenate([right[0], right[1], right[0]], 0),
                (((0,), (0,)), ((), ())),
                preferred_element_type=f32,
            )
            for i in range(2 * t + 2, 16):
                rows[i] = jnp.where(own, 0.0, rows[i]) - update[8 * i : 8 * i + 8, :]
    return jnp.concatenate(rows, 0)


def eliminate(work):
    size = work.shape[0]
    lane = lax.broadcasted_iota(jnp.int32, (B, B), 1)
    sub = lax.broadcasted_iota(jnp.int32, (B, B), 0)
    for done in range(0, size, B):
        rows = slice(done, done + B)
        w = jnp.where(lane <= sub, inverse_factor(work[rows, rows]), 0.0)
        new = dot3(split(w), split(work[rows, :]))
        work[rows, :] = new
        work[rows, rows] = w
        if done + B == size:
            break
        turned_high, turned_low = split(work[rows, done + B :].T)
        high, low = split(work[rows, :])
        for start in range(done + B, size, B):
            at = slice(start - done - B, start - done)
            left = (turned_high[at], turned_low[at])
            target = slice(start, start + B)
            x = dot3(left, (high[:, : done + B], low[:, : done + B]))
            if done:
                work[target, :done] = work[target, :done] - x[:, :done]
            work[target, rows] = -x[:, done:]
            y = dot3(left, (high[:, start:], low[:, start:]))
            work[target, start:] = work[target, start:] - y


def factor_body(c, tokens, members, *refs):
    last = c == CHUNKS - 1
    slab, member = slab_member(members)
    if c in EARLY:
        share_refs = refs[:CHUNKS]
        *before, out_ref, work, rows_ref = refs[CHUNKS:]
        first = 0 if c == EARLY[-1] else tile_count(range(c))
        for steps, ref in enumerate(share_refs):
            x = lax.rem(slab + (CHUNKS - steps), CHUNKS)
            for index, (block, group, tile) in enumerate(tiles_of(c)):
                row = pl.multiple_of(8 * x + (block * B + 8 * CHUNKS * group), 8)
                rows_ref[pl.ds(row, 8), tile * B : (tile + 1) * B] = ref[first + index]
        for block in range(W // B):
            for other in range(block):
                rows = slice(block * B, (block + 1) * B)
                at = c * W + other * B
                low = rows_ref[rows, at : at + B]
                rows_ref[other * B : (other + 1) * B, c * W + block * B : c * W + (block + 1) * B] = low.T
    else:
        late_ref, *before, out_ref, work, rows_ref, semaphore = refs
        first = sum(late + 1 for late in LATE if late < c) * W
        copy = pltpu.make_async_copy(
            late_ref.at[:, first : first + (c + 1) * W], rows_ref, semaphore
        )
        copy.start()
        copy.wait()
    lane = lax.broadcasted_iota(jnp.int32, (W, W), 1)
    sub = lax.broadcasted_iota(jnp.int32, (W, W), 0)
    scale = 1.0 / tokens
    block = rows_ref[:, c * W :] * scale + jnp.where(lane == sub, DAMPING, 0.0)
    parts = []
    if c:
        row = split(rows_ref[:, : c * W] * scale)
        halves = [split(ref[...]) for ref in before]
        for j in range(c):
            size = (j + 1) * W
            part = dot3_nt((row[0][:, :size], row[1][:, :size]), halves[j])
            parts.append(split(part))
            block = block - dot3_nt(parts[j], parts[j])
    work[...] = block
    eliminate(work)
    if not last:
        own = jnp.where(lane <= sub, work[...], 0.0)
        out_ref[:, c * W :] = own
    else:
        count = out_ref.shape[1]
        start = pl.multiple_of(member * count, 8)
        own_lane = lax.broadcasted_iota(jnp.int32, (count, W), 1)
        own_row = lax.broadcasted_iota(jnp.int32, (count, W), 0) + start
        own = jnp.where(own_lane <= own_row, work[pl.ds(start, count), :], 0.0)

    def left_of_own():
        own_halves = split(own)
        sums = [None] * c
        for j in range(c):
            ahead = split(dot3(own_halves, parts[j]))
            for i in range(j + 1):
                at = slice(i * W, (i + 1) * W)
                term = dot3(ahead, (halves[j][0][:, at], halves[j][1][:, at]))
                sums[i] = term if sums[i] is None else sums[i] + term
        return sums

    if not last:
        if c:
            for i, total in enumerate(left_of_own()):
                out_ref[:, i * W : (i + 1) * W] = -total
        return

    for j in range(c):

        @pl.when(slab == j)
        def _():
            size = (j + 1) * W
            out_ref[0, :, :size] = before[j][pl.ds(start, count), :]
            out_ref[0, :, size:] = jnp.zeros((count, BLK - size), f32)

    @pl.when(slab == c)
    def _():
        for i, total in enumerate(left_of_own()):
            out_ref[0, :, i * W : (i + 1) * W] = -total
        out_ref[0, :, c * W :] = own


def factor(c, shares, before, tokens, members):
    shape = (1, W // members, BLK) if c == CHUNKS - 1 else (W, (c + 1) * W)
    vmem = pl.BlockSpec(memory_space=pltpu.VMEM)
    scratch = [pltpu.VMEM((W, W), f32), pltpu.VMEM((W, (c + 1) * W), f32)]
    if c in EARLY:
        in_specs = [vmem] * len(shares)
    else:
        in_specs = [pl.BlockSpec(memory_space=pl.ANY)]
        scratch.append(pltpu.SemaphoreType.DMA)
    return pl.pallas_call(
        lambda *refs: factor_body(c, tokens, members, *refs),
        out_shape=jax.ShapeDtypeStruct(shape, f32),
        in_specs=in_specs + [vmem] * c,
        out_specs=vmem,
        scratch_shapes=scratch,
        compiler_params=pltpu.CompilerParams(vmem_limit_bytes=VMEM),
        cost_estimate=pl.CostEstimate(
            flops=10_000_000_000 if c == 1 else 100_000_000,
            bytes_accessed=8 * W * W * (c + 1),
            transcendentals=0,
        ),
    )(*shares, *before)


def on_device(embedded, out_grads, section_gains, plan):
    data_count = lax.axis_size("dp")
    micro, rows, _ = embedded.shape
    slab = data_count // CHUNKS
    along = [[z + slab * x for z in range(slab)] for x in range(CHUNKS)]
    gains = lax.all_gather(section_gains, "pipe", axis=0)
    normed, left, right = relay(plan, embedded, gains, out_grads)

    def along_slab(tiles, steps):
        pairs = [
            (z + slab * x, (z + steps) % slab + slab * x)
            for x in range(CHUNKS)
            for z in range(slab)
        ]
        return lax.ppermute(tiles, "dp", pairs)

    def from_slabs(tiles):
        shares = [tiles]
        for steps in range(1, CHUNKS):
            pairs = [
                (z + slab * x, z + slab * ((x + steps) % CHUNKS))
                for z in range(slab)
                for x in range(CHUNKS)
            ]
            shares.append(lax.ppermute(tiles, "dp", pairs))
        return shares

    lefts = from_slabs(left)
    right, early = covariance(lefts, right, slab)
    rights = from_slabs(right)
    late = late_covariance(lefts, rights)
    early = fold(lax.all_to_all(early, "dp", 0, 0, axis_index_groups=along), late)
    early, middle = lay([early] + [along_slab(early, k) for k in range(1, slab)])
    late = lax.psum(late, "dp", axis_index_groups=along)

    tokens = micro * rows * data_count
    early = from_slabs(early)
    middle = from_slabs(later(middle, early[1:]))
    before = []
    for c, shares in zip(range(CHUNKS), (early, early, middle, [late])):
        before.append(factor(c, shares, before, tokens, slab))
    return normed, before[-1]


def solution(mesh):
    in_specs = (P(None, "dp", None), P("pipe", None, "dp", None), P("pipe", None), P())
    out_specs = (P("pipe", None, "dp", None), P("pipe", "dp", None))
    return jax.shard_map(
        on_device, mesh=mesh, in_specs=in_specs, out_specs=out_specs, check_vma=False
    )
```
